32 devices in a mesh: groups: 1, expert: 32 (over z, y, x, core).
Axes of the slice: x: 2, y: 2, z: 4, core: 2. Of those that a mesh axis runs over, the one named last changes fastest.
Arguments:
- tokens: bfloat16 [4096, 2048], P(('groups', 'expert')), may hold values from -6 to 6
- cotangent: bfloat16 [4096, 2048], P(('groups', 'expert')), may hold values from -6 to 6
- token_experts: int32 [4096, 6], P(('groups', 'expert')), may hold values from 0 to 15, all different within a row; in each aligned block of 128 rows (0 to 127, 128 to 255, ...) at most 56 rows name the same one
- routing_weight_cache: float32 [4096, 6], P(('groups', 'expert')), may hold values from 0.05 to 0.5
- gate_weight: bfloat16 [32, 2048, 352], P('expert'), may hold values from -0.125 to 0.125
- up_weight: bfloat16 [32, 2048, 352], P('expert'), may hold values from -0.125 to 0.125
- down_weight: bfloat16 [32, 352, 2048], P('expert'), may hold values from -0.21875 to 0.21875
- gate_adapter_input: bfloat16 [32, 1024, 64], P('expert'), may hold values from -0.125 to 0.125
- gate_adapter_output: bfloat16 [32, 64, 352], P('expert'), may hold values from -0.75 to 0.75
- up_adapter_input: bfloat16 [32, 1024, 64], P('expert'), may hold values from -0.125 to 0.125
- up_adapter_output: bfloat16 [32, 64, 352], P('expert'), may hold values from -0.75 to 0.75
Outputs:
- grad_tokens: bfloat16 [4096, 2048], P(('groups', 'expert'))
- grad_a_gate: float32 [32, 1024, 64], P(('groups', 'expert'))
- grad_b_gate: float32 [32, 64, 352], P(('groups', 'expert'))
- grad_a_up: float32 [32, 1024, 64], P(('groups', 'expert'))
- grad_b_up: float32 [32, 64, 352], P(('groups', 'expert'))
The draws below stay inside these ranges and needn't reach their ends.
Inputs may be any that keep to these rules, and one draw needn't show every extreme that they name: `token_experts`: each row names 6 different experts; within the 128 rows of one device no expert is named more than 56 times.
All inputs are finite; a program needn't handle non-finite values.
Results may differ from the reference program's by a relative error of at most 0.0066.
Values may be sent and summed in bfloat16 or wider, within the bound.
A program may use at most 128 MiB of HBM per device.

```python
import math
import jax
import jax.numpy as jnp
import numpy as np
from jax import lax

MODEL_WIDTH = 2048
EXPERT_HIDDEN = 704
ADAPTER_RANK = 64
TOP = 6
TOK_DEV = 128
ACTIVE_EXPERTS = 16
EXPERT_HALVES = 32
CAP = 56
HALF_MODEL_WIDTH = 1024
HALF_HIDDEN = 352
TOKENS = 4096
N_EXPERT = 32


def shard_levels(stream_key, dims, cuts, least, largest):
    loudness = 1.0
    for position, shards_of in cuts:
        steps = jax.random.uniform(jax.random.fold_in(jax.random.fold_in(stream_key, 6), position), (shards_of,), jnp.float32, least / len(cuts), largest / len(cuts))
        loudness = loudness * jnp.repeat(jnp.exp(steps), dims[position] // shards_of).reshape((-1,) + (1,) * (len(dims) - 1 - position))
    return loudness


def shared_out(key, own, number, rows, amount, top, reach, slope):
    order = jax.random.permutation(key, amount)
    packed, usual = portions_of(amount, rows * top, reach, slope, True), portions_of(amount, rows * top, reach, slope, False)
    places = jnp.arange(amount)

    def named(lengths, rotation):
        used = int((lengths > 0).sum())
        fixed = max(1, used // 4)
        moved = fixed + (places - fixed + rotation * (used - fixed)) % max(1, amount - fixed)
        return jnp.zeros((amount,), jnp.int32).at[order[jnp.where(places < fixed, places, moved)]].set(jnp.asarray(lengths, jnp.int32))

    lengths = jnp.where(number % 4 == 0, named(packed, number // 4), named(usual, number - number // 4 - 1))
    mixed = jax.random.permutation(jax.random.fold_in(own, 3), amount)
    donor, taker = mixed[0:amount // 2 * 2:2], mixed[1:amount // 2 * 2:2]
    room = jnp.minimum(lengths[donor] - 1, reach - lengths[taker]) // 2
    room = jnp.where((donor == order[0]) | (taker == order[0]) | (lengths[taker] == 0), 0, jnp.maximum(room, 0))
    moved = jax.random.randint(jax.random.fold_in(own, 4), (amount // 2,), 0, 1 << 20) % (room + 1)
    lengths = lengths.at[donor].add(-moved).at[taker].add(moved)
    items = jnp.searchsorted(jnp.cumsum(lengths), jnp.arange(rows * top), side="right").astype(jnp.int32)
    table = items.reshape(top, rows).T
    table = table[jax.random.permutation(jax.random.fold_in(own, 1), rows)]
    rotation = jax.random.randint(jax.random.fold_in(own, 2), (rows, 1), 0, top)
    return jnp.take_along_axis(table, (jnp.arange(top)[None, :] + rotation) % top, axis=1)


def portions_of(amount, total, limit, lean, full):
    weights = [(1 << 20) // math.isqrt(grade ** lean) + 1 for grade in range(1, amount + 1)]
    largest = limit if full else min(limit, max(-(-total // amount), total * weights[0] // sum(weights)))
    least = 1 if total - largest >= amount - 1 else 0
    holding, rest = [largest] + [least] * (amount - 1), total - largest - least * (amount - 1)
    while rest > 0:
        candidates = [i for i in range(1, amount) if holding[i] < largest] or [i for i in range(1, amount) if holding[i] < limit]
        whole, remaining = sum([weights[i] for i in candidates]), rest
        for i in candidates:
            more = min(limit - holding[i], max(1, remaining * weights[i] // whole), rest)
            holding[i] = holding[i] + more
            rest = rest - more
    return np.array(holding)


def noise(key, shape, scale, bound, cuts=(), kind=jnp.bfloat16):
    entries = jax.random.normal(key, shape, jnp.float32) * scale
    if len(cuts) > 0:
        entries = shard_levels(key, shape, cuts, -0.22, 0.18) * entries
    return jnp.clip(entries, min=-bound, max=bound).astype(kind)


def setup_inputs(seed: int = 0, part: int = 0) -> dict:
    key_of = jax.random.split(jax.random.key(seed), 12)
    part_keys = jax.random.split(jax.random.fold_in(key_of[11], part), 12)
    tokens = noise(part_keys[0], (TOKENS, MODEL_WIDTH), 1.0, 6.0, ((0, 32),))
    cotangent = noise(part_keys[1], (TOKENS, MODEL_WIDTH), 1.0, 6.0, ((0, 32),))
    token_experts_keys = jax.random.split(jax.random.fold_in(part_keys[2], 1), TOKENS // TOK_DEV)
    token_experts_turns = jax.random.permutation(jax.random.fold_in(part_keys[2], 3), TOKENS // TOK_DEV)
    token_experts = jax.vmap(lambda own, number: shared_out(jax.random.fold_in(part_keys[2], 2), own, number, TOK_DEV, ACTIVE_EXPERTS, TOP, CAP, 1))(token_experts_keys, token_experts_turns).reshape((TOKENS, TOP))
    routing_weight_cache = jnp.clip(jnp.exp(math.log(0.5) - 2.3025851 * jax.random.uniform(part_keys[3], (TOKENS, TOP), jnp.float32) ** shard_levels(part_keys[3], (TOKENS, TOP), ((0, 32),), -0.2, 0.2)), 0.05, 0.5)
    gate_weight = noise(key_of[4], (EXPERT_HALVES, MODEL_WIDTH, HALF_HIDDEN), MODEL_WIDTH ** -0.5, 0.125, ((0, 32),))
    up_weight = noise(key_of[5], (EXPERT_HALVES, MODEL_WIDTH, HALF_HIDDEN), MODEL_WIDTH ** -0.5, 0.125, ((0, 32),))
    down_weight = noise(key_of[6], (EXPERT_HALVES, HALF_HIDDEN, MODEL_WIDTH), EXPERT_HIDDEN ** -0.5, 0.21875, ((0, 32),))
    gate_adapter_input = noise(key_of[7], (EXPERT_HALVES, HALF_MODEL_WIDTH, ADAPTER_RANK), MODEL_WIDTH ** -0.5, 0.125, ((0, 32),))
    gate_adapter_output = noise(key_of[8], (EXPERT_HALVES, ADAPTER_RANK, HALF_HIDDEN), ADAPTER_RANK ** -0.5, 0.75, ((0, 32),))
    up_adapter_input = noise(key_of[9], (EXPERT_HALVES, HALF_MODEL_WIDTH, ADAPTER_RANK), MODEL_WIDTH ** -0.5, 0.125, ((0, 32),))
    up_adapter_output = noise(key_of[10], (EXPERT_HALVES, ADAPTER_RANK, HALF_HIDDEN), ADAPTER_RANK ** -0.5, 0.75, ((0, 32),))
    return dict(tokens=tokens, cotangent=cotangent, token_experts=token_experts, routing_weight_cache=routing_weight_cache, gate_weight=gate_weight, up_weight=up_weight, down_weight=down_weight, gate_adapter_input=gate_adapter_input, gate_adapter_output=gate_adapter_output, up_adapter_input=up_adapter_input, up_adapter_output=up_adapter_output)


def slot_places(token_experts, expert_count, slot_cap):
    flat_ids = token_experts.reshape(-1)
    picks = (flat_ids[:, None] == jnp.arange(expert_count, dtype=jnp.int32)[None, :]).astype(jnp.int32)
    earlier = jnp.cumsum(picks, axis=0) - picks
    slots = jnp.sum(earlier * picks, axis=1)
    return (flat_ids * slot_cap + slots).astype(jnp.int32).reshape(token_experts.shape)


def merge_hidden(pieces):
    count, inner, width = pieces.shape
    return pieces.reshape(count // 2, 2, inner, width).transpose(0, 2, 1, 3).reshape(count // 2, inner, 2 * width)


def split_hidden(whole):
    count, inner, width = whole.shape
    return whole.reshape(count, inner, 2, width // 2).transpose(0, 2, 1, 3).reshape(2 * count, inner, width // 2)


def expert_backward(operands):
    rows_x, rows_dy, gate_w, up_w, down_w, a_gate, b_gate, a_up, b_up = operands
    rank = a_gate.shape[1]
    low_rank = jnp.dot(rows_x, jnp.concatenate([a_gate, a_up], axis=1), preferred_element_type=jnp.float32).astype(jnp.bfloat16)
    low_gate = low_rank[:, :rank]
    low_up = low_rank[:, rank:]
    gate = jnp.dot(rows_x, gate_w, preferred_element_type=jnp.float32) + jnp.dot(low_gate, b_gate, preferred_element_type=jnp.float32)
    upward = jnp.dot(rows_x, up_w, preferred_element_type=jnp.float32) + jnp.dot(low_up, b_up, preferred_element_type=jnp.float32)
    hidden_grad = jnp.dot(rows_dy, down_w.T, preferred_element_type=jnp.float32)
    sigmoid_gate = jax.nn.sigmoid(gate)
    grad_gate = (hidden_grad * upward * sigmoid_gate * (1.0 + gate * (1.0 - sigmoid_gate))).astype(jnp.bfloat16)
    grad_up = (hidden_grad * gate * sigmoid_gate).astype(jnp.bfloat16)
    back_gate = jnp.dot(grad_gate, b_gate.T, preferred_element_type=jnp.float32).astype(jnp.bfloat16)
    back_up = jnp.dot(grad_up, b_up.T, preferred_element_type=jnp.float32).astype(jnp.bfloat16)
    row_grads = (jnp.dot(grad_gate, gate_w.T, preferred_element_type=jnp.float32)
                 + jnp.dot(grad_up, up_w.T, preferred_element_type=jnp.float32)
                 + jnp.dot(back_gate, a_gate.T, preferred_element_type=jnp.float32)
                 + jnp.dot(back_up, a_up.T, preferred_element_type=jnp.float32))
    grad_ag = jnp.dot(rows_x.T, back_gate, preferred_element_type=jnp.float32)
    grad_bg = jnp.dot(low_gate.T, grad_gate, preferred_element_type=jnp.float32)
    grad_au = jnp.dot(rows_x.T, back_up, preferred_element_type=jnp.float32)
    grad_bu = jnp.dot(low_up.T, grad_up, preferred_element_type=jnp.float32)
    return row_grads, grad_ag, grad_bg, grad_au, grad_bu


def block_places(block_ids):
    return slot_places(block_ids, ACTIVE_EXPERTS, CAP)


def collect_rows(block_rows, block_place):
    return jnp.sum(block_rows[block_place.reshape(-1)].reshape(TOK_DEV, TOP, MODEL_WIDTH), axis=1)


def by_expert(sent):
    return sent.reshape(N_EXPERT, ACTIVE_EXPERTS, CAP, MODEL_WIDTH).transpose(1, 0, 2, 3).reshape(ACTIVE_EXPERTS, N_EXPERT * CAP, MODEL_WIDTH)


def reference(tokens, cotangent, token_experts, routing_weight_cache, gate_weight, up_weight, down_weight, gate_adapter_input, gate_adapter_output, up_adapter_input, up_adapter_output):
    x_blocks = tokens.reshape(N_EXPERT, TOK_DEV, MODEL_WIDTH)
    places = jax.vmap(block_places)(token_experts.reshape(N_EXPERT, TOK_DEV, TOP))
    scaled = (routing_weight_cache[:, :, None] * cotangent[:, None, :].astype(jnp.float32)).astype(jnp.bfloat16)
    scaled = scaled.reshape(N_EXPERT, TOK_DEV, TOP, MODEL_WIDTH)
    x_copies = jnp.broadcast_to(x_blocks[:, :, None, :], (N_EXPERT, TOK_DEV, TOP, MODEL_WIDTH))
    sources = jnp.broadcast_to(jnp.arange(N_EXPERT, dtype=jnp.int32)[:, None, None], places.shape)
    empty = jnp.zeros((N_EXPERT, ACTIVE_EXPERTS * CAP, MODEL_WIDTH), jnp.bfloat16)
    sent_x = empty.at[sources, places].set(x_copies)
    sent_dy = empty.at[sources, places].set(scaled)
    operands = (by_expert(sent_x), by_expert(sent_dy), merge_hidden(gate_weight), merge_hidden(up_weight),
                down_weight.reshape(ACTIVE_EXPERTS, EXPERT_HIDDEN, MODEL_WIDTH), gate_adapter_input.reshape(ACTIVE_EXPERTS, MODEL_WIDTH, ADAPTER_RANK), merge_hidden(gate_adapter_output),
                up_adapter_input.reshape(ACTIVE_EXPERTS, MODEL_WIDTH, ADAPTER_RANK), merge_hidden(up_adapter_output))
    row_grads, grad_ag, grad_bg, grad_au, grad_bu = lax.map(expert_backward, operands)
    returned = row_grads.reshape(ACTIVE_EXPERTS, N_EXPERT, CAP, MODEL_WIDTH).transpose(1, 0, 2, 3).reshape(N_EXPERT, ACTIVE_EXPERTS * CAP, MODEL_WIDTH)
    grad_tokens = jax.vmap(collect_rows)(returned, places).reshape(TOKENS, MODEL_WIDTH).astype(jnp.bfloat16)
    return (grad_tokens, grad_ag.reshape(N_EXPERT, HALF_MODEL_WIDTH, ADAPTER_RANK), split_hidden(grad_bg),
            grad_au.reshape(N_EXPERT, HALF_MODEL_WIDTH, ADAPTER_RANK), split_hidden(grad_bu))
```

```python
import jax
import jax.numpy as jnp
from jax import lax
from jax.sharding import PartitionSpec as P


def swapped(value, axis, distance):
    mask = 2**distance
    pairs = [(source, source ^ mask) for source in range(lax.axis_size(axis))]
    return lax.ppermute(value, axis, pairs)


def slot_places(token_experts, expert_count, slot_cap):
    flat_ids = token_experts.reshape(-1)
    picks = (flat_ids[:, None] == jnp.arange(expert_count, dtype=jnp.int32)[None, :]).astype(
        jnp.int32
    )
    earlier = jnp.cumsum(picks, axis=0) - picks
    slots = jnp.sum(earlier * picks, axis=1)
    return (flat_ids * slot_cap + slots).reshape(token_experts.shape)


def trans_right(left, right):
    return lax.dot_general(
        left, right, (((1,), (1,)), ((), ())), preferred_element_type=jnp.float32
    )


def trans_left(left, right):
    return lax.dot_general(
        left, right, (((0,), (0,)), ((), ())), preferred_element_type=jnp.float32
    )


def joined(own, axis, my_half):
    other = swapped(own, "expert", 0)
    first = jnp.where(my_half == 0, own, other)
    second = jnp.where(my_half == 0, other, own)
    return jnp.concatenate([first, second], axis=axis)


def half_sum(whole, axis, my_half):
    size = whole.shape[axis] // 2
    kept = lax.dynamic_slice_in_dim(whole, my_half * size, size, axis)
    given = lax.dynamic_slice_in_dim(whole, (1 - my_half) * size, size, axis)
    return kept + swapped(given, "expert", 0)


def expert_rows(rows_x, rows_dy, params, my_half):
    gate_w, up_w, down_w, adapters, b_gate, b_up = params
    rank = b_gate.shape[0]
    low_rank = jnp.dot(rows_x, adapters, preferred_element_type=jnp.float32).astype(jnp.bfloat16)
    low_gate = low_rank[:, :rank]
    low_up = low_rank[:, rank:]
    gate = jnp.dot(rows_x, gate_w, preferred_element_type=jnp.float32) + jnp.dot(
        low_gate, b_gate, preferred_element_type=jnp.float32
    )
    upward = jnp.dot(rows_x, up_w, preferred_element_type=jnp.float32) + jnp.dot(
        low_up, b_up, preferred_element_type=jnp.float32
    )
    hidden_grad = trans_right(rows_dy, down_w)
    sigmoid_gate = jax.nn.sigmoid(gate)
    grad_gate = (hidden_grad * upward * sigmoid_gate * (1.0 + gate * (1.0 - sigmoid_gate))).astype(
        jnp.bfloat16
    )
    grad_up = (hidden_grad * gate * sigmoid_gate).astype(jnp.bfloat16)
    back = jnp.concatenate(
        [trans_right(grad_gate, b_gate), trans_right(grad_up, b_up)], axis=1
    ).astype(jnp.bfloat16)
    row_grads = (
        trans_right(grad_gate, gate_w) + trans_right(grad_up, up_w) + trans_right(back, adapters)
    ).astype(jnp.bfloat16)
    grad_adapter = half_sum(trans_left(rows_x, back), 0, my_half)
    grad_b = jnp.stack([trans_left(low_gate, grad_gate), trans_left(low_up, grad_up)])
    grad_b = half_sum(grad_b, 2, my_half)
    return (row_grads, (grad_adapter[:, :rank], grad_b[0], grad_adapter[:, rank:], grad_b[1]))


def on_device(
    tokens,
    cotangent,
    token_experts,
    routing_weight_cache,
    gate_weight,
    up_weight,
    down_weight,
    gate_adapter_input,
    gate_adapter_output,
    up_adapter_input,
    up_adapter_output,
):
    n_devices = lax.axis_size("expert")
    n_experts = n_devices // 2
    tok_count, width = tokens.shape
    top_count = token_experts.shape[1]
    slot_cap = 2 * max(2, 9 * tok_count * top_count // (16 * n_experts) + 1)
    slot_total = n_experts * slot_cap
    my_half = lax.axis_index("expert") % 2
    same_half = [list(range(half, n_devices, 2)) for half in range(2)]
    places = slot_places(token_experts, n_experts, slot_cap)
    picker = places[None, :, :] == jnp.arange(slot_total, dtype=jnp.int32)[:, None, None]
    pick_mask = jnp.any(picker, axis=2)
    token_pick = pick_mask.astype(jnp.bfloat16)
    slot_weight = jnp.sum(jnp.where(picker, routing_weight_cache[None, :, :], 0.0), axis=(1, 2))
    send_x = jnp.dot(token_pick, tokens, preferred_element_type=jnp.float32).astype(jnp.bfloat16)
    send_dy = (
        jnp.dot(token_pick, cotangent, preferred_element_type=jnp.float32) * slot_weight[:, None]
    ).astype(jnp.bfloat16)
    params = (
        joined(gate_weight[0], 1, my_half),
        joined(up_weight[0], 1, my_half),
        joined(down_weight[0], 0, my_half),
        joined(jnp.concatenate([gate_adapter_input[0], up_adapter_input[0]], axis=1), 0, my_half),
        joined(gate_adapter_output[0], 1, my_half),
        joined(up_adapter_output[0], 1, my_half),
    )

    def exchanged(rows):
        return lax.all_to_all(
            rows.reshape(n_experts, slot_cap, width),
            "expert",
            split_axis=0,
            concat_axis=0,
            tiled=True,
            axis_index_groups=same_half,
        ).reshape(slot_total, width)

    row_grads, grads = expert_rows(exchanged(send_x), exchanged(send_dy), params, my_half)
    returned = exchanged(row_grads)
    grad_tokens = trans_left(token_pick, returned).astype(jnp.bfloat16)
    grad_ag, grad_bg, grad_au, grad_bu = grads
    return (grad_tokens, grad_ag[None], grad_bg[None], grad_au[None], grad_bu[None])


def solution(mesh):
    in_specs = (
        P(("groups", "expert"), None),
        P(("groups", "expert"), None),
        P(("groups", "expert"), None),
        P(("groups", "expert"), None),
        P("expert", None, None),
        P("expert", None, None),
        P("expert", None, None),
        P("expert", None, None),
        P("expert", None, None),
        P("expert", None, None),
        P("expert", None, None),
    )
    out_specs = (
        P(("groups", "expert"), None),
        P(("groups", "expert"), None, None),
        P(("groups", "expert"), None, None),
        P(("groups", "expert"), None, None),
        P(("groups", "expert"), None, None),
    )
    return jax.shard_map(
        on_device, mesh=mesh, in_specs=in_specs, out_specs=out_specs, check_vma=False
    )
```

```python
import functools

import jax
import jax.numpy as jnp
from jax import lax
from jax.experimental import pallas as pl
from jax.experimental.pallas import tpu as pltpu
from jax.sharding import PartitionSpec as P

PLANE = 4
ANY = pl.BlockSpec(memory_space=pl.ANY)
VMEM = pl.BlockSpec(memory_space=pltpu.VMEM)


def trans_right(left, right):
    return lax.dot_general(
        left, right, (((1,), (1,)), ((), ())), preferred_element_type=jnp.float32
    )


def trans_left(left, right):
    return lax.dot_general(
        left, right, (((0,), (0,)), ((), ())), preferred_element_type=jnp.float32
    )


def position(planes):
    me = lax.axis_index("expert")
    half = lax.rem(me, 2)
    chip = lax.div(me, 2)
    return lax.div(chip, PLANE), lax.rem(chip, PLANE), half


def device(z, q, half):
    return {"expert": (z * PLANE + q) * 2 + half}


def remote(src, dst, send, recv, target):
    return pltpu.make_async_remote_copy(
        src_ref=src,
        dst_ref=dst,
        send_sem=send,
        recv_sem=recv,
        device_id=target,
        device_id_type=pl.DeviceIdType.MESH,
    )


def greet(target):
    pl.semaphore_signal(
        pltpu.get_barrier_semaphore(),
        inc=1,
        device_id=target,
        device_id_type=pl.DeviceIdType.MESH,
    )


def dispatch_kernel(
    planes,
    experts,
    cap,
    x_ref,
    c_ref,
    meta_ref,
    *refs,
):
    pieces = refs[:5]
    rows_ref, metas_ref = refs[5:7]
    others = refs[7:12]
    zbuf, zmeta, stage, load_sem, w_send, w_recv = refs[12:18]
    up_send, down_send, z_recv, um_send, dm_send, m_recv, p_send, p_recv, own_sem = refs[18:]
    z, q, half = position(planes)
    tok, width = x_ref.shape
    last = planes - 1

    own_x = pltpu.make_async_copy(x_ref, zbuf.at[z, pl.ds(0, tok)], load_sem.at[0])
    own_c = pltpu.make_async_copy(c_ref, zbuf.at[z, pl.ds(tok, tok)], load_sem.at[1])
    own_x.start()
    own_c.start()
    zmeta[z] = meta_ref[...]

    greet(device(z, q, 1 - half))
    for step in range(1, PLANE):
        greet(device(z, lax.rem(q + step, PLANE), half))

    @pl.when(z < last)
    def _():
        greet(device(z + 1, q, half))

    @pl.when(z > 0)
    def _():
        greet(device(z - 1, q, half))

    near = jnp.where(z < last, 1, 0) + jnp.where(z > 0, 1, 0)
    pl.semaphore_wait(pltpu.get_barrier_semaphore(), PLANE + near)
    own_x.wait()
    own_c.wait()

    def up(b):
        target = device(z + 1, q, half)
        return (
            remote(zmeta.at[b], zmeta.at[b], um_send.at[b], m_recv.at[b], target),
            remote(zbuf.at[b], zbuf.at[b], up_send.at[b], z_recv.at[b], target),
        )

    def down(b):
        target = device(z - 1, q, half)
        return (
            remote(zmeta.at[b], zmeta.at[b], dm_send.at[b], m_recv.at[b], target),
            remote(zbuf.at[b], zbuf.at[b], down_send.at[b], z_recv.at[b], target),
        )

    def begin(copies):
        for copy in copies:
            copy.start()

    def arrived(copies):
        for copy in copies:
            copy.wait_recv()

    def sent(copies):
        for copy in copies:
            copy.wait_send()

    def piece(i):
        return remote(
            pieces[i], others[i], w_send.at[i], w_recv.at[i], device(z, q, 1 - half)
        )

    def part(b, to):
        return remote(
            stage.at[b, to],
            rows_ref.at[q, b],
            p_send.at[b, to],
            p_recv.at[q, b],
            device(z, to, half),
        )

    def came(b, source):
        return remote(
            stage.at[b, source],
            rows_ref.at[source, b],
            p_send.at[b, source],
            p_recv.at[source, b],
            device(z, source, half),
        )

    def local(b):
        return pltpu.make_async_copy(stage.at[b, q], rows_ref.at[q, b], own_sem.at[b])

    def picked(b, to):
        expert = z * PLANE + to
        slots = zmeta[b, pl.ds(expert, 1), :]
        weights = zmeta[b, pl.ds(experts + expert, 1), :]
        numbers = lax.broadcasted_iota(jnp.int32, (cap, tok), 0).astype(jnp.float32)
        mask = numbers == slots
        ones = jnp.where(mask, 1.0, 0.0)
        zeros = jnp.zeros_like(ones)
        scale = jnp.sum(jnp.where(mask, weights, 0.0), axis=1, keepdims=True)
        scale = jnp.concatenate([jnp.ones_like(scale), scale], axis=0)
        picker = jnp.concatenate(
            [
                jnp.concatenate([ones, zeros], axis=1),
                jnp.concatenate([zeros, ones], axis=1),
            ],
            axis=0,
        ).astype(jnp.bfloat16)
        tile = width // 4
        for n in range(4):
            cols = pl.ds(n * tile, tile)
            rows = jnp.dot(picker, zbuf[b, :, cols], preferred_element_type=jnp.float32)
            stage[b, to, :, cols] = (rows * scale).astype(jnp.bfloat16)

    def spread(b):
        def one(step, carry):
            to = lax.rem(q + step, PLANE)
            picked(b, to)
            part(b, to).start()
            return carry

        lax.fori_loop(1, PLANE, one, 0)
        picked(b, q)
        local(b).start()

    @pl.when(z < last)
    def _():
        begin(up(z))

    @pl.when(z > 0)
    def _():
        begin(down(z))

    for i in range(5):
        piece(i).start()
    spread(z)

    def step(k, carry):
        below, above = z - k, z + k

        @pl.when(below >= 0)
        def _():
            arrived(down(below))

            @pl.when(z < last)
            def _():
                begin(up(below))

        @pl.when(above <= last)
        def _():
            arrived(up(above))

            @pl.when(z > 0)
            def _():
                begin(down(above))

        @pl.when(below >= 0)
        def _():
            spread(below)

        @pl.when(above <= last)
        def _():
            spread(above)

        return carry

    lax.fori_loop(1, planes, step, 0)
    metas_ref[...] = zmeta[...]

    def finish(b, carry):
        def one(step, inner):
            to = lax.rem(q + step, PLANE)
            part(b, to).wait_send()
            came(b, to).wait_recv()
            return inner

        lax.fori_loop(1, PLANE, one, 0)
        local(b).wait()

        @pl.when((b <= z) & (z < last))
        def _():
            sent(up(b))

        @pl.when((b >= z) & (z > 0))
        def _():
            sent(down(b))

        return carry

    lax.fori_loop(0, planes, finish, 0)
    for i in range(5):
        piece(i).wait()


def dispatch(planes, experts, cap, tokens, cotangent, meta, pieces):
    tok, width = tokens.shape
    bf16, f32 = jnp.bfloat16, jnp.float32
    dma = pltpu.SemaphoreType.DMA
    shape = jax.ShapeDtypeStruct
    return pl.pallas_call(
        functools.partial(dispatch_kernel, planes, experts, cap),
        out_shape=[
            shape((PLANE, planes, 2 * cap, width), bf16),
            shape((planes,) + meta.shape, f32),
        ]
        + [shape(piece.shape, piece.dtype) for piece in pieces],
        in_specs=[ANY, ANY, VMEM] + [ANY] * len(pieces),
        out_specs=[ANY, VMEM] + [ANY] * len(pieces),
        scratch_shapes=[
            pltpu.VMEM((planes, 2 * tok, width), bf16),
            pltpu.VMEM((planes,) + meta.shape, f32),
            pltpu.VMEM((planes, PLANE, 2 * cap, width), bf16),
            dma((2,)),
            dma((len(pieces),)),
            dma((len(pieces),)),
            dma((planes,)),
            dma((planes,)),
            dma((planes,)),
            dma((planes,)),
            dma((planes,)),
            dma((planes,)),
            dma((planes, PLANE)),
            dma((PLANE, planes)),
            dma((planes,)),
        ],
        compiler_params=pltpu.CompilerParams(
            collective_id=0, has_side_effects=True, vmem_limit_bytes=40 * 2**20
        ),
        name="dispatch",
    )(tokens, cotangent, meta, *pieces)


CHUNKS = 4


def combine_kernel(
    planes,
    y_ref,
    pick_ref,
    keep_a,
    give_a,
    keep_b,
    give_b,
    out_ref,
    sum_a,
    sum_b,
    ybuf,
    stage,
    zin,
    got_a,
    got_b,
    y_send,
    y_recv,
    own_sem,
    z_send,
    z_recv,
    g_send,
    g_recv,
):
    z, q, half = position(planes)
    tok, width = out_ref.shape
    tile = width // CHUNKS

    greet(device(z, q, 1 - half))
    for step in range(1, PLANE):
        greet(device(z, lax.rem(q + step, PLANE), half))

    def hello(step, carry):
        greet(device(lax.rem(z + step, planes), q, half))
        return carry

    lax.fori_loop(1, planes, hello, 0)
    pl.semaphore_wait(pltpu.get_barrier_semaphore(), PLANE + planes - 1)

    def cols(j):
        return pl.ds(pl.multiple_of(j * tile, tile), tile)

    def give(j, to):
        return remote(
            y_ref.at[to, :, cols(j)],
            ybuf.at[q, :, cols(j)],
            y_send.at[j, to],
            y_recv.at[j, q],
            device(z, to, half),
        )

    def came(j, source):
        return remote(
            y_ref.at[source, :, cols(j)],
            ybuf.at[source, :, cols(j)],
            y_send.at[j, source],
            y_recv.at[j, source],
            device(z, source, half),
        )

    def local(j):
        return pltpu.make_async_copy(
            y_ref.at[q, :, cols(j)], ybuf.at[q, :, cols(j)], own_sem.at[j]
        )

    def part(j, to):
        return remote(
            stage.at[to, :, cols(j)],
            zin.at[z, :, cols(j)],
            z_send.at[j, to],
            z_recv.at[j, z],
            device(to, q, half),
        )

    def part_came(j, source):
        return remote(
            stage.at[source, :, cols(j)],
            zin.at[source, :, cols(j)],
            z_send.at[j, source],
            z_recv.at[j, source],
            device(source, q, half),
        )

    partner = device(z, q, 1 - half)
    grads = (
        remote(give_a, got_a, g_send.at[0], g_recv.at[0], partner),
        remote(give_b, got_b, g_send.at[1], g_recv.at[1], partner),
    )

    def send(j, carry):
        def one(step, inner):
            give(j, lax.rem(q + step, PLANE)).start()
            return inner

        lax.fori_loop(1, PLANE, one, 0)
        local(j).start()
        return carry

    lax.fori_loop(0, CHUNKS, send, 0)
    for copy in grads:
        copy.start()

    def work(j, carry):
        def one(step, inner):
            came(j, lax.rem(q + step, PLANE)).wait_recv()
            return inner

        lax.fori_loop(1, PLANE, one, 0)
        local(j).wait()
        for target in range(planes):
            rows = pl.ds(target * tok, tok)
            total = jnp.zeros((tok, tile), jnp.float32)
            for source in range(PLANE):
                total += jnp.dot(
                    pick_ref[source, rows, :],
                    ybuf[source, :, cols(j)],
                    preferred_element_type=jnp.float32,
                )
            stage[target, :, cols(j)] = total.astype(jnp.bfloat16)

        def post(step, inner):
            part(j, lax.rem(z + step, planes)).start()
            return inner

        lax.fori_loop(1, planes, post, 0)
        return carry

    lax.fori_loop(0, CHUNKS, work, 0)

    for copy in grads:
        copy.wait()
    sum_a[...] = keep_a[...] + got_a[...]
    sum_b[...] = keep_b[...] + got_b[...]

    def gather(j, carry):
        def one(step, total):
            source = lax.rem(z + step, planes)
            part_came(j, source).wait_recv()
            return total + zin[source, :, cols(j)].astype(jnp.float32)

        total = lax.fori_loop(1, planes, one, stage[z, :, cols(j)].astype(jnp.float32))
        out_ref[:, cols(j)] = total.astype(jnp.bfloat16)
        return carry

    lax.fori_loop(0, CHUNKS, gather, 0)

    def finish(j, carry):
        def one(step, inner):
            give(j, lax.rem(q + step, PLANE)).wait_send()
            return inner

        def two(step, inner):
            part(j, lax.rem(z + step, planes)).wait_send()
            return inner

        lax.fori_loop(1, PLANE, one, 0)
        lax.fori_loop(1, planes, two, 0)
        return carry

    lax.fori_loop(0, CHUNKS, finish, 0)


def combine(planes, tok, y, pick, keep_a, give_a, keep_b, give_b):
    width = y.shape[2]
    bf16, f32 = jnp.bfloat16, jnp.float32
    dma = pltpu.SemaphoreType.DMA
    shape = jax.ShapeDtypeStruct
    return pl.pallas_call(
        functools.partial(combine_kernel, planes),
        out_shape=[
            shape((tok, width), bf16),
            shape(keep_a.shape, f32),
            shape(keep_b.shape, f32),
        ],
        in_specs=[ANY, VMEM, VMEM, VMEM, VMEM, VMEM],
        out_specs=[VMEM, VMEM, VMEM],
        scratch_shapes=[
            pltpu.VMEM(y.shape, bf16),
            pltpu.VMEM((planes, tok, width), bf16),
            pltpu.VMEM((planes, tok, width), bf16),
            pltpu.VMEM(keep_a.shape, f32),
            pltpu.VMEM(keep_b.shape, f32),
            dma((CHUNKS, PLANE)),
            dma((CHUNKS, PLANE)),
            dma((CHUNKS,)),
            dma((CHUNKS, planes)),
            dma((CHUNKS, planes)),
            dma((2,)),
            dma((2,)),
        ],
        compiler_params=pltpu.CompilerParams(
            collective_id=1, has_side_effects=True, vmem_limit_bytes=40 * 2**20
        ),
        name="combine",
    )(y, pick, keep_a, give_a, keep_b, give_b)


def expert_rows(rows_x, rows_dy, own, other, my_half):
    adapter_own, adapter_other = own[3], other[3]
    rank = own[4].shape[0] // 2
    adapters = jnp.where(
        my_half == 0,
        jnp.concatenate([adapter_own, adapter_other], axis=0),
        jnp.concatenate([adapter_other, adapter_own], axis=0),
    )
    low_rank = jnp.dot(rows_x, adapters, preferred_element_type=jnp.float32).astype(jnp.bfloat16)
    low_gate = low_rank[:, :rank]
    low_up = low_rank[:, rank:]
    row_grads = 0.0
    back = 0.0
    grads_b = []
    for gate_w, up_w, down_w, _, b_out in (own, other):
        b_gate, b_up = b_out[:rank], b_out[rank:]
        gate = jnp.dot(rows_x, gate_w, preferred_element_type=jnp.float32) + jnp.dot(
            low_gate, b_gate, preferred_element_type=jnp.float32
        )
        upward = jnp.dot(rows_x, up_w, preferred_element_type=jnp.float32) + jnp.dot(
            low_up, b_up, preferred_element_type=jnp.float32
        )
        hidden_grad = trans_right(rows_dy, down_w)
        sigmoid_gate = jax.nn.sigmoid(gate)
        grad_gate = (
            hidden_grad * upward * sigmoid_gate * (1.0 + gate * (1.0 - sigmoid_gate))
        ).astype(jnp.bfloat16)
        grad_up = (hidden_grad * gate * sigmoid_gate).astype(jnp.bfloat16)
        back += jnp.concatenate(
            [trans_right(grad_gate, b_gate), trans_right(grad_up, b_up)], axis=1
        )
        row_grads += trans_right(grad_gate, gate_w) + trans_right(grad_up, up_w)
        grads_b.append(jnp.stack([trans_left(low_gate, grad_gate), trans_left(low_up, grad_up)]))
    back = back.astype(jnp.bfloat16)
    row_grads = (row_grads + trans_right(back, adapters)).astype(jnp.bfloat16)
    return row_grads, trans_left(rows_x, back), grads_b


def on_device(
    tokens,
    cotangent,
    token_experts,
    routing_weight_cache,
    gate_weight,
    up_weight,
    down_weight,
    gate_adapter_input,
    gate_adapter_output,
    up_adapter_input,
    up_adapter_output,
):
    n_devices = lax.axis_size("expert")
    n_experts = n_devices // 2
    planes = n_experts // PLANE
    tok, width = tokens.shape
    top = token_experts.shape[1]
    rank = gate_adapter_input.shape[2]
    slot_cap = 2 * max(2, 9 * tok * top // (16 * n_experts) + 1)
    slot_cap = (slot_cap + 7) // 8 * 8
    my_z, _, my_half = position(planes)

    named = token_experts[None, :, :] == jnp.arange(n_experts, dtype=jnp.int32)[:, None, None]
    chosen = jnp.any(named, axis=2).astype(jnp.float32)
    earlier = (
        lax.broadcasted_iota(jnp.int32, (tok, tok), 0)
        < lax.broadcasted_iota(jnp.int32, (tok, tok), 1)
    ).astype(jnp.float32)
    slots = jnp.dot(chosen, earlier, preferred_element_type=jnp.float32)
    slots = jnp.where(chosen > 0, slots, -1.0)
    weights = jnp.sum(jnp.where(named, routing_weight_cache[None, :, :], 0.0), axis=2)
    meta = jnp.concatenate([slots, weights], axis=0)

    own = (
        gate_weight[0],
        up_weight[0],
        down_weight[0],
        jnp.concatenate([gate_adapter_input[0], up_adapter_input[0]], axis=1),
        jnp.concatenate([gate_adapter_output[0], up_adapter_output[0]], axis=0),
    )
    rows, metas, *other = dispatch(planes, n_experts, slot_cap, tokens, cotangent, meta, own)
    rows_x = rows[:, :, :slot_cap].reshape(-1, width)
    rows_dy = rows[:, :, slot_cap:].reshape(-1, width)
    row_grads, grad_a, grads_b = expert_rows(rows_x, rows_dy, own, other, my_half)

    plane_slots = lax.dynamic_slice_in_dim(metas, my_z * PLANE, PLANE, 1)
    same = jnp.eye(planes, dtype=jnp.bool_)[None, :, None, :, None]
    hit = plane_slots.transpose(1, 0, 2)[:, :, :, None, None] == jnp.arange(
        slot_cap, dtype=jnp.float32
    )
    pick = (same & hit).astype(jnp.bfloat16).reshape(PLANE, planes * tok, planes * slot_cap)

    half_width = grad_a.shape[0] // 2
    keep_a = lax.dynamic_slice_in_dim(grad_a, my_half * half_width, half_width, 0)
    give_a = lax.dynamic_slice_in_dim(grad_a, (1 - my_half) * half_width, half_width, 0)
    grad_tokens, sum_a, sum_b = combine(
        planes,
        tok,
        row_grads.reshape(PLANE, planes * slot_cap, width),
        pick,
        keep_a,
        give_a,
        grads_b[0],
        grads_b[1],
    )
    return (
        grad_tokens,
        sum_a[None, :, :rank],
        sum_b[None, 0],
        sum_a[None, :, rank:],
        sum_b[None, 1],
    )


def solution(mesh):
    in_specs = (
        P(("groups", "expert"), None),
        P(("groups", "expert"), None),
        P(("groups", "expert"), None),
        P(("groups", "expert"), None),
        P("expert", None, None),
        P("expert", None, None),
        P("expert", None, None),
        P("expert", None, None),
        P("expert", None, None),
        P("expert", None, None),
        P("expert", None, None),
    )
    out_specs = (
        P(("groups", "expert"), None),
        P(("groups", "expert"), None, None),
        P(("groups", "expert"), None, None),
        P(("groups", "expert"), None, None),
        P(("groups", "expert"), None, None),
    )
    return jax.shard_map(
        on_device, mesh=mesh, in_specs=in_specs, out_specs=out_specs, check_vma=False
    )
```

```python
import functools

import jax
import jax.numpy as jnp
from jax import lax
from jax.experimental import pallas as pl
from jax.experimental.pallas import tpu as pltpu
from jax.sharding import PartitionSpec as P

PLANE = 4
ANY = pl.BlockSpec(memory_space=pl.ANY)
VMEM = pl.BlockSpec(memory_space=pltpu.VMEM)


def trans_right(left, right):
    return lax.dot_general(
        left, right, (((1,), (1,)), ((), ())), preferred_element_type=jnp.float32
    )


def trans_left(left, right):
    return lax.dot_general(
        left, right, (((0,), (0,)), ((), ())), preferred_element_type=jnp.float32
    )


def position(planes):
    me = lax.axis_index("expert")
    half = lax.rem(me, 2)
    chip = lax.div(me, 2)
    return lax.div(chip, PLANE), lax.rem(chip, PLANE), half


def device(z, q, half):
    return {"expert": (z * PLANE + q) * 2 + half}


def remote(src, dst, send, recv, target):
    return pltpu.make_async_remote_copy(
        src_ref=src,
        dst_ref=dst,
        send_sem=send,
        recv_sem=recv,
        device_id=target,
        device_id_type=pl.DeviceIdType.MESH,
    )


def greet(target):
    pl.semaphore_signal(
        pltpu.get_barrier_semaphore(),
        inc=1,
        device_id=target,
        device_id_type=pl.DeviceIdType.MESH,
    )


def layer_kernel(
    planes,
    experts,
    cap,
    x_ref,
    c_ref,
    meta_ref,
    wg_ref,
    wu_ref,
    wd_ref,
    ag_ref,
    au_ref,
    bt_ref,
    out_ref,
    sum_ag,
    sum_au,
    sum_b,
    zbuf,
    zmeta,
    stage,
    rows,
    pickers,
    wg,
    wu,
    wd,
    at,
    bt,
    xs,
    ds,
    gg,
    gu,
    acc_a,
    acc_b,
    got_a,
    got_b,
    y,
    ybuf,
    zstage,
    zin,
    load_sem,
    w_load,
    w_send,
    w_recv,
    up_send,
    down_send,
    z_recv,
    um_send,
    dm_send,
    m_recv,
    p_send,
    p_recv,
    own_sem,
    y_send,
    y_recv,
    y_own,
    s_send,
    s_recv,
    g_send,
    g_recv,
):
    z, q, half = position(planes)
    tok, width = x_ref.shape
    wide = width // 2
    hidden_half = wg_ref.shape[0]
    hidden = 2 * hidden_half
    rank = ag_ref.shape[0]
    count = PLANE * cap
    last = planes - 1
    partner = device(z, q, 1 - half)

    own_x = pltpu.make_async_copy(x_ref, zbuf.at[z, pl.ds(0, tok)], load_sem.at[0])
    own_c = pltpu.make_async_copy(c_ref, zbuf.at[z, pl.ds(tok, tok)], load_sem.at[1])
    own_x.start()
    own_c.start()
    zmeta[z] = meta_ref[...]

    mine = pl.ds(pl.multiple_of(half * hidden_half, hidden_half), hidden_half)
    pieces = (
        (bt_ref, bt.at[mine]),
        (ag_ref, at.at[half, pl.ds(0, rank)]),
        (au_ref, at.at[half, pl.ds(rank, rank)]),
        (wg_ref, wg.at[mine]),
        (wu_ref, wu.at[mine]),
        (wd_ref, wd.at[mine]),
    )

    def piece_local(i):
        return pltpu.make_async_copy(pieces[i][0], pieces[i][1], w_load.at[i])

    def piece(i):
        return remote(pieces[i][0], pieces[i][1], w_send.at[i], w_recv.at[i], partner)

    for i in range(len(pieces)):
        piece_local(i).start()

    greet(partner)

    def hello_plane(step, carry):
        greet(device(z, lax.rem(q + step, PLANE), half))
        return carry

    def hello_column(step, carry):
        greet(device(lax.rem(z + step, planes), q, half))
        return carry

    lax.fori_loop(1, PLANE, hello_plane, 0)
    lax.fori_loop(1, planes, hello_column, 0)
    pl.semaphore_wait(pltpu.get_barrier_semaphore(), PLANE + planes - 1)
    own_x.wait()
    own_c.wait()

    def up(b):
        target = device(z + 1, q, half)
        return (
            remote(zmeta.at[b], zmeta.at[b], um_send.at[b], m_recv.at[b], target),
            remote(zbuf.at[b], zbuf.at[b], up_send.at[b], z_recv.at[b], target),
        )

    def down(b):
        target = device(z - 1, q, half)
        return (
            remote(zmeta.at[b], zmeta.at[b], dm_send.at[b], m_recv.at[b], target),
            remote(zbuf.at[b], zbuf.at[b], down_send.at[b], z_recv.at[b], target),
        )

    def begin(copies):
        for copy in copies:
            copy.start()

    def arrived(copies):
        for copy in copies:
            copy.wait_recv()

    def sent(copies):
        for copy in copies:
            copy.wait_send()

    def part(b, to):
        return remote(
            stage.at[b, to],
            rows.at[b, q],
            p_send.at[b, to],
            p_recv.at[b, q],
            device(z, to, half),
        )

    def part_came(b, source):
        return remote(
            stage.at[b, source],
            rows.at[b, source],
            p_send.at[b, source],
            p_recv.at[b, source],
            device(z, source, half),
        )

    def part_local(b):
        return pltpu.make_async_copy(stage.at[b, q], rows.at[b, q], own_sem.at[b])

    def give(b, to):
        return remote(
            y.at[b, to],
            ybuf.at[b, q],
            y_send.at[b, to],
            y_recv.at[b, q],
            device(z, to, half),
        )

    def give_came(b, source):
        return remote(
            y.at[b, source],
            ybuf.at[b, source],
            y_send.at[b, source],
            y_recv.at[b, source],
            device(z, source, half),
        )

    def give_local(b):
        return pltpu.make_async_copy(y.at[b, q], ybuf.at[b, q], y_own.at[b])

    def home(to):
        return remote(
            zstage.at[to], zin.at[z], s_send.at[to], s_recv.at[z], device(to, q, half)
        )

    def home_came(source):
        return remote(
            zstage.at[source],
            zin.at[source],
            s_send.at[source],
            s_recv.at[source],
            device(source, q, half),
        )

    def block_at(i):
        near = 2 * jnp.minimum(z, last - z)
        odd = lax.rem(i, 2)
        step = lax.div(i + odd, 2)
        around = jnp.where(odd == 1, z - step, z + step)
        onward = jnp.where(2 * z <= last, i, last - i)
        return jnp.where(i <= near, around, onward)

    def picked(b, to):
        expert = z * PLANE + to
        slots = zmeta[b, pl.ds(expert, 1), :]
        weights = zmeta[b, pl.ds(experts + expert, 1), :]
        numbers = lax.broadcasted_iota(jnp.int32, (cap, tok), 0).astype(jnp.float32)
        mask = numbers == slots
        ones = jnp.where(mask, 1.0, 0.0)
        zeros = jnp.zeros_like(ones)
        scale = jnp.sum(jnp.where(mask, weights, 0.0), axis=1, keepdims=True)
        scale = jnp.concatenate([jnp.ones_like(scale), scale], axis=0)
        picker = jnp.concatenate(
            [
                jnp.concatenate([ones, zeros], axis=1),
                jnp.concatenate([zeros, ones], axis=1),
            ],
            axis=0,
        ).astype(jnp.bfloat16)
        pickers[b, to] = picker
        tile = width // 4
        for n in range(4):
            cols = pl.ds(n * tile, tile)
            found = jnp.dot(picker, zbuf[b, :, cols], preferred_element_type=jnp.float32)
            stage[b, to, :, cols] = (found * scale).astype(jnp.bfloat16)

    def spread(i):
        b = block_at(i)

        @pl.when(b < z)
        def _():
            arrived(down(b))

            @pl.when(z < last)
            def _():
                begin(up(b))

        @pl.when(b > z)
        def _():
            arrived(up(b))

            @pl.when(z > 0)
            def _():
                begin(down(b))

        def one(step, carry):
            to = lax.rem(q + step, PLANE)
            picked(b, to)
            part(b, to).start()
            return carry

        lax.fori_loop(1, PLANE, one, 0)
        picked(b, q)
        part_local(b).start()

    def expert(i):
        b = block_at(i)

        def one(step, carry):
            part_came(b, lax.rem(q + step, PLANE)).wait_recv()
            return carry

        lax.fori_loop(1, PLANE, one, 0)
        part_local(b).wait()
        f32, bf16 = jnp.float32, jnp.bfloat16
        for n in range(4):
            cols = pl.ds(n * (width // 4), width // 4)
            both = [rows[b, source, :, cols].astype(f32) for source in range(PLANE)]
            xs[:, cols] = jnp.concatenate([v[:cap] for v in both], axis=0).astype(bf16)
            ds[:, cols] = jnp.concatenate([v[cap:] for v in both], axis=0).astype(bf16)
        low = (
            trans_right(xs[:, :wide], at[0]) + trans_right(xs[:, wide:], at[1])
        ).astype(bf16)
        lanes = lax.broadcasted_iota(jnp.int32, (count, 2 * rank), 1)
        low_gate = jnp.where(lanes < rank, low, jnp.zeros_like(low))
        low_up = jnp.where(lanes < rank, jnp.zeros_like(low), low)
        for lo in range(0, hidden, 256):
            hi = min(lo + 256, hidden)
            gate = trans_right(xs[...], wg[lo:hi]) + trans_right(low_gate, bt[lo:hi])
            upward = trans_right(xs[...], wu[lo:hi]) + trans_right(low_up, bt[lo:hi])
            hidden_grad = trans_right(ds[...], wd[lo:hi])
            sig = 1.0 / (1.0 + jnp.exp(-gate))
            gg[:, lo:hi] = (hidden_grad * upward * sig * (1.0 + gate * (1.0 - sig))).astype(bf16)
            gu[:, lo:hi] = (hidden_grad * gate * sig).astype(bf16)
        back = jnp.where(
            lanes < rank,
            jnp.dot(gg[...], bt[...], preferred_element_type=f32),
            jnp.dot(gu[...], bt[...], preferred_element_type=f32),
        ).astype(bf16)
        tile = wide // 4

        def columns(t, carry):
            sides = []
            for side in range(2):
                cols = pl.ds(pl.multiple_of(side * wide + t * tile, tile), tile)
                inner = pl.ds(pl.multiple_of(t * tile, tile), tile)
                sides.append(
                    jnp.dot(gg[...], wg[:, cols], preferred_element_type=f32)
                    + jnp.dot(gu[...], wu[:, cols], preferred_element_type=f32)
                    + jnp.dot(back, at[side, :, inner], preferred_element_type=f32)
                )
            for source in range(PLANE):
                these = slice(source * cap, (source + 1) * cap)
                y[b, source, :, inner] = jnp.concatenate(
                    [side[these] for side in sides], axis=0
                ).astype(bf16)
            return carry

        lax.fori_loop(0, 4, columns, 0)

        def send(step, carry):
            give(b, lax.rem(q + step, PLANE)).start()
            return carry

        lax.fori_loop(1, PLANE, send, 0)
        give_local(b).start()
        for n in range(4):
            cols = pl.ds(n * (width // 4), width // 4)
            acc_a[:, cols] += trans_left(back, xs[:, cols])
        of_b = lax.broadcasted_iota(jnp.int32, (hidden, 2 * rank), 1)
        acc_b[...] += jnp.where(of_b < rank, trans_left(gg[...], low), trans_left(gu[...], low))

    def collect(i):
        b = block_at(i)

        def one(step, carry):
            give_came(b, lax.rem(q + step, PLANE)).wait_recv()
            return carry

        lax.fori_loop(1, PLANE, one, 0)
        give_local(b).wait()
        picker = pickers[b].reshape(PLANE * 2 * cap, 2 * tok)
        tile = wide // 2
        for n in range(2):
            cols = pl.ds(n * tile, tile)
            held = ybuf[b, :, :, cols].reshape(PLANE * 2 * cap, tile)
            zstage[b, :, cols] = trans_left(picker, held).astype(jnp.bfloat16)

        @pl.when(b != z)
        def _():
            home(b).start()

    @pl.when(z < last)
    def _():
        begin(up(z))

    @pl.when(z > 0)
    def _():
        begin(down(z))

    for i in range(len(pieces)):
        piece(i).start()
    acc_a[...] = jnp.zeros_like(acc_a)
    acc_b[...] = jnp.zeros_like(acc_b)

    def step(i, carry):
        @pl.when(i < planes)
        def _():
            spread(i)

        @pl.when(i == 1)
        def _():
            for n in range(len(pieces)):
                piece_local(n).wait()
                piece(n).wait()

        @pl.when((i >= 1) & (i <= planes))
        def _():
            expert(i - 1)

        @pl.when(i >= 2)
        def _():
            collect(i - 2)

        return carry

    lax.fori_loop(0, planes + 2, step, 0)

    theirs = pl.ds(pl.multiple_of((1 - half) * hidden_half, hidden_half), hidden_half)
    other_cols = pl.ds(pl.multiple_of((1 - half) * wide, wide), wide)
    own_cols = pl.ds(pl.multiple_of(half * wide, wide), wide)
    grads = (
        remote(acc_a.at[:, other_cols], got_a, g_send.at[0], g_recv.at[0], partner),
        remote(acc_b.at[theirs], got_b, g_send.at[1], g_recv.at[1], partner),
    )
    for copy in grads:
        copy.start()
    for copy in grads:
        copy.wait()
    total_a = acc_a[:, own_cols] + got_a[...]
    sum_ag[...] = total_a[:rank]
    sum_au[...] = total_a[rank:]
    sum_b[...] = acc_b[mine] + got_b[...]

    def add(step, total):
        source = lax.rem(z + step, planes)
        home_came(source).wait_recv()
        return total + zin[source].astype(jnp.float32)

    total = lax.fori_loop(1, planes, add, zstage[z].astype(jnp.float32))
    out_ref[:, :wide] = total[:tok].astype(jnp.bfloat16)
    out_ref[:, wide:] = total[tok:].astype(jnp.bfloat16)

    def finish(b, carry):
        def one(step, inner):
            to = lax.rem(q + step, PLANE)
            part(b, to).wait_send()
            give(b, to).wait_send()
            return inner

        lax.fori_loop(1, PLANE, one, 0)

        @pl.when((b <= z) & (z < last))
        def _():
            sent(up(b))

        @pl.when((b >= z) & (z > 0))
        def _():
            sent(down(b))

        @pl.when(b != z)
        def _():
            home(b).wait_send()

        return carry

    lax.fori_loop(0, planes, finish, 0)


def layer(planes, experts, cap, tokens, cotangent, meta, pieces):
    tok, width = tokens.shape
    hidden_half = pieces[0].shape[0]
    rank = pieces[3].shape[0]
    hidden, wide, count = 2 * hidden_half, width // 2, PLANE * cap
    bf16, f32 = jnp.bfloat16, jnp.float32
    dma = pltpu.SemaphoreType.DMA
    shape = jax.ShapeDtypeStruct
    per_block, per_pair, six = dma((planes,)), dma((planes, PLANE)), dma((len(pieces),))
    return pl.pallas_call(
        functools.partial(layer_kernel, planes, experts, cap),
        out_shape=[
            shape((tok, width), bf16),
            shape((rank, wide), f32),
            shape((rank, wide), f32),
            shape((hidden_half, 2 * rank), f32),
        ],
        in_specs=[ANY, ANY, VMEM] + [ANY] * len(pieces),
        out_specs=[VMEM] * 4,
        scratch_shapes=[
            pltpu.VMEM((planes, 2 * tok, width), bf16),
            pltpu.VMEM((planes,) + meta.shape, f32),
            pltpu.VMEM((planes, PLANE, 2 * cap, width), bf16),
            pltpu.VMEM((planes, PLANE, 2 * cap, width), bf16),
            pltpu.VMEM((planes, PLANE, 2 * cap, 2 * tok), bf16),
            pltpu.VMEM((hidden, width), bf16),
            pltpu.VMEM((hidden, width), bf16),
            pltpu.VMEM((hidden, width), bf16),
            pltpu.VMEM((2, 2 * rank, wide), bf16),
            pltpu.VMEM((hidden, 2 * rank), bf16),
            pltpu.VMEM((count, width), bf16),
            pltpu.VMEM((count, width), bf16),
            pltpu.VMEM((count, hidden), bf16),
            pltpu.VMEM((count, hidden), bf16),
            pltpu.VMEM((2 * rank, width), f32),
            pltpu.VMEM((hidden, 2 * rank), f32),
            pltpu.VMEM((2 * rank, wide), f32),
            pltpu.VMEM((hidden_half, 2 * rank), f32),
            pltpu.VMEM((planes, PLANE, 2 * cap, wide), bf16),
            pltpu.VMEM((planes, PLANE, 2 * cap, wide), bf16),
            pltpu.VMEM((planes, 2 * tok, wide), bf16),
            pltpu.VMEM((planes, 2 * tok, wide), bf16),
            dma((2,)),
            six,
            six,
            six,
        ]
        + [per_block] * 6
        + [per_pair, per_pair, per_block]
        + [per_pair, per_pair, per_block]
        + [per_block, per_block, dma((2,)), dma((2,))],
        compiler_params=pltpu.CompilerParams(
            collective_id=0, has_side_effects=True, vmem_limit_bytes=62 * 2**20
        ),
        name="layer",
    )(tokens, cotangent, meta, *pieces)


def on_device(
    tokens,
    cotangent,
    token_experts,
    routing_weight_cache,
    gate_weight,
    up_weight,
    down_weight,
    gate_adapter_input,
    gate_adapter_output,
    up_adapter_input,
    up_adapter_output,
):
    n_devices = lax.axis_size("expert")
    n_experts = n_devices // 2
    planes = n_experts // PLANE
    tok, width = tokens.shape
    top = token_experts.shape[1]
    slot_cap = 2 * max(2, 9 * tok * top // (16 * n_experts) + 1)
    slot_cap = (slot_cap + 7) // 8 * 8
    rank = gate_adapter_input.shape[2]

    named = token_experts[None, :, :] == jnp.arange(n_experts, dtype=jnp.int32)[:, None, None]
    chosen = jnp.any(named, axis=2).astype(jnp.float32)
    earlier = (
        lax.broadcasted_iota(jnp.int32, (tok, tok), 0)
        < lax.broadcasted_iota(jnp.int32, (tok, tok), 1)
    ).astype(jnp.float32)
    slots = jnp.dot(chosen, earlier, preferred_element_type=jnp.float32)
    slots = jnp.where(chosen > 0, slots, -1.0)
    weights = jnp.sum(jnp.where(named, routing_weight_cache[None, :, :], 0.0), axis=2)
    meta = jnp.concatenate([slots, weights], axis=0)

    pieces = (
        gate_weight[0].T,
        up_weight[0].T,
        down_weight[0],
        gate_adapter_input[0].T,
        up_adapter_input[0].T,
        jnp.concatenate([gate_adapter_output[0], up_adapter_output[0]], axis=0).T,
    )
    grad_tokens, sum_ag, sum_au, sum_b = layer(
        planes, n_experts, slot_cap, tokens, cotangent, meta, pieces
    )
    return (
        grad_tokens,
        sum_ag.T[None],
        sum_b[:, :rank].T[None],
        sum_au.T[None],
        sum_b[:, rank:].T[None],
    )


def solution(mesh):
    in_specs = (
        P(("groups", "expert"), None),
        P(("groups", "expert"), None),
        P(("groups", "expert"), None),
        P(("groups", "expert"), None),
        P("expert", None, None),
        P("expert", None, None),
        P("expert", None, None),
        P("expert", None, None),
        P("expert", None, None),
        P("expert", None, None),
        P("expert", None, None),
    )
    out_specs = (
        P(("groups", "expert"), None),
        P(("groups", "expert"), None, None),
        P(("groups", "expert"), None, None),
        P(("groups", "expert"), None, None),
        P(("groups", "expert"), None, None),
    )
    return jax.shard_map(
        on_device, mesh=mesh, in_specs=in_specs, out_specs=out_specs, check_vma=False
    )
```

```python
import functools

import jax
import jax.numpy as jnp
from jax import lax
from jax.experimental import pallas as pl
from jax.experimental.pallas import tpu as pltpu
from jax.sharding import PartitionSpec as P

PLANE = 4
ANY = pl.BlockSpec(memory_space=pl.ANY)
VMEM = pl.BlockSpec(memory_space=pltpu.VMEM)


def trans_right(left, right):
    return lax.dot_general(
        left, right, (((1,), (1,)), ((), ())), preferred_element_type=jnp.float32
    )


def trans_left(left, right):
    return lax.dot_general(
        left, right, (((0,), (0,)), ((), ())), preferred_element_type=jnp.float32
    )


def position(planes):
    me = lax.axis_index("expert")
    half = lax.rem(me, 2)
    chip = lax.div(me, 2)
    return lax.div(chip, PLANE), lax.rem(chip, PLANE), half


def device(z, q, half):
    return {"expert": (z * PLANE + q) * 2 + half}


def remote(src, dst, send, recv, target):
    return pltpu.make_async_remote_copy(
        src_ref=src,
        dst_ref=dst,
        send_sem=send,
        recv_sem=recv,
        device_id=target,
        device_id_type=pl.DeviceIdType.MESH,
    )


def greet(target):
    pl.semaphore_signal(
        pltpu.get_barrier_semaphore(),
        inc=1,
        device_id=target,
        device_id_type=pl.DeviceIdType.MESH,
    )


def layer_kernel(
    planes,
    experts,
    cap,
    x_ref,
    c_ref,
    meta_ref,
    wg_ref,
    wu_ref,
    wd_ref,
    ag_ref,
    au_ref,
    bt_ref,
    out_ref,
    sum_ag,
    sum_au,
    sum_bg,
    sum_bu,
    zbuf,
    zmeta,
    stage,
    rows,
    pickers,
    wg,
    wu,
    wd,
    at,
    bt,
    xs,
    ds,
    gg,
    gu,
    acc_a,
    acc_b,
    got_a,
    got_b,
    y,
    ybuf,
    zstage,
    zin,
    load_sem,
    w_load,
    w_send,
    w_recv,
    up_send,
    down_send,
    z_recv,
    um_send,
    dm_send,
    m_recv,
    p_send,
    p_recv,
    own_sem,
    y_send,
    y_recv,
    y_own,
    s_send,
    s_recv,
    g_send,
    g_recv,
):
    z, q, half = position(planes)
    tok, width = x_ref.shape
    wide = width // 2
    hidden_half = wg_ref.shape[0]
    hidden = 2 * hidden_half
    rank = ag_ref.shape[0]
    count = PLANE * cap
    last = planes - 1
    partner = device(z, q, 1 - half)

    own_x = pltpu.make_async_copy(x_ref, zbuf.at[z, pl.ds(0, tok)], load_sem.at[0])
    own_c = pltpu.make_async_copy(c_ref, zbuf.at[z, pl.ds(tok, tok)], load_sem.at[1])
    own_x.start()
    own_c.start()
    zmeta[z] = meta_ref[...]

    mine = pl.ds(pl.multiple_of(half * hidden_half, hidden_half), hidden_half)
    pieces = (
        (bt_ref, bt.at[mine]),
        (ag_ref, at.at[half, pl.ds(0, rank)]),
        (au_ref, at.at[half, pl.ds(rank, rank)]),
        (wg_ref, wg.at[mine]),
        (wu_ref, wu.at[mine]),
        (wd_ref, wd.at[mine]),
    )

    def piece_local(i):
        return pltpu.make_async_copy(pieces[i][0], pieces[i][1], w_load.at[i])

    def piece(i):
        return remote(pieces[i][0], pieces[i][1], w_send.at[i], w_recv.at[i], partner)

    for i in range(len(pieces)):
        piece_local(i).start()

    greet(partner)

    def hello_plane(step, carry):
        greet(device(z, lax.rem(q + step, PLANE), half))
        return carry

    def hello_column(step, carry):
        greet(device(lax.rem(z + step, planes), q, half))
        return carry

    lax.fori_loop(1, PLANE, hello_plane, 0)
    lax.fori_loop(1, planes, hello_column, 0)
    pl.semaphore_wait(pltpu.get_barrier_semaphore(), PLANE + planes - 1)
    own_x.wait()
    own_c.wait()

    def up(b):
        target = device(z + 1, q, half)
        return (
            remote(zmeta.at[b], zmeta.at[b], um_send.at[b], m_recv.at[b], target),
            remote(zbuf.at[b], zbuf.at[b], up_send.at[b], z_recv.at[b], target),
        )

    def down(b):
        target = device(z - 1, q, half)
        return (
            remote(zmeta.at[b], zmeta.at[b], dm_send.at[b], m_recv.at[b], target),
            remote(zbuf.at[b], zbuf.at[b], down_send.at[b], z_recv.at[b], target),
        )

    def begin(copies):
        for copy in copies:
            copy.start()

    def arrived(copies):
        for copy in copies:
            copy.wait_recv()

    def sent(copies):
        for copy in copies:
            copy.wait_send()

    def part(b, to):
        return remote(
            stage.at[b, to],
            rows.at[b, q],
            p_send.at[b, to],
            p_recv.at[b, q],
            device(z, to, half),
        )

    def part_came(b, source):
        return remote(
            stage.at[b, source],
            rows.at[b, source],
            p_send.at[b, source],
            p_recv.at[b, source],
            device(z, source, half),
        )

    def part_local(b):
        return pltpu.make_async_copy(stage.at[b, q], rows.at[b, q], own_sem.at[b])

    def give(b, to):
        return remote(
            y.at[b, to],
            ybuf.at[b, q],
            y_send.at[b, to],
            y_recv.at[b, q],
            device(z, to, half),
        )

    def give_came(b, source):
        return remote(
            y.at[b, source],
            ybuf.at[b, source],
            y_send.at[b, source],
            y_recv.at[b, source],
            device(z, source, half),
        )

    def give_local(b):
        return pltpu.make_async_copy(y.at[b, q], ybuf.at[b, q], y_own.at[b])

    def home(to):
        return remote(
            zstage.at[to], zin.at[z], s_send.at[to], s_recv.at[z], device(to, q, half)
        )

    def home_came(source):
        return remote(
            zstage.at[source],
            zin.at[source],
            s_send.at[source],
            s_recv.at[source],
            device(source, q, half),
        )

    def block_at(i):
        near = 2 * jnp.minimum(z, last - z)
        odd = lax.rem(i, 2)
        step = lax.div(i + odd, 2)
        low = 2 * z <= last
        around = jnp.where((odd == 1) == low, z + step, z - step)
        onward = jnp.where(low, i, last - i)
        return jnp.where(i <= near, around, onward)

    def picked(b, to):
        expert = z * PLANE + to
        slots = zmeta[b, pl.ds(expert, 1), :]
        weights = zmeta[b, pl.ds(experts + expert, 1), :]
        numbers = lax.broadcasted_iota(jnp.int32, (cap, tok), 0).astype(jnp.float32)
        mask = numbers == slots
        ones = jnp.where(mask, 1.0, 0.0)
        zeros = jnp.zeros_like(ones)
        scale = jnp.sum(jnp.where(mask, weights, 0.0), axis=1, keepdims=True)
        scale = jnp.concatenate([jnp.ones_like(scale), scale], axis=0)
        picker = jnp.concatenate(
            [
                jnp.concatenate([ones, zeros], axis=1),
                jnp.concatenate([zeros, ones], axis=1),
            ],
            axis=0,
        ).astype(jnp.bfloat16)
        pickers[b, to] = picker
        tile = width // 4
        for n in range(4):
            cols = pl.ds(n * tile, tile)
            found = jnp.dot(picker, zbuf[b, :, cols], preferred_element_type=jnp.float32)
            stage[b, to, :, cols] = (found * scale).astype(jnp.bfloat16)

    def forward(i):
        below, above = z - i, z + i

        @pl.when(below >= 0)
        def _():
            arrived(down(below))

            @pl.when(z < last)
            def _():
                begin(up(below))

        @pl.when(above <= last)
        def _():
            arrived(up(above))

            @pl.when(z > 0)
            def _():
                begin(down(above))

    def spread(i):
        b = block_at(i)

        def one(step, carry):
            to = lax.rem(q + step, PLANE)
            picked(b, to)
            part(b, to).start()
            return carry

        lax.fori_loop(1, PLANE, one, 0)
        picked(b, q)
        part_local(b).start()

    def answer(b):
        def send(step, carry):
            give(b, lax.rem(q + step, PLANE)).start()
            return carry

        lax.fori_loop(1, PLANE, send, 0)
        give_local(b).start()

    def expert(i):
        b = block_at(i)

        def one(step, carry):
            part_came(b, lax.rem(q + step, PLANE)).wait_recv()
            return carry

        lax.fori_loop(1, PLANE, one, 0)
        part_local(b).wait()
        f32, bf16 = jnp.float32, jnp.bfloat16
        for n in range(4):
            cols = pl.ds(n * (width // 4), width // 4)
            both = [rows[b, source, :, cols].astype(f32) for source in range(PLANE)]
            xs[:, cols] = jnp.concatenate([v[:cap] for v in both], axis=0).astype(bf16)
            ds[:, cols] = jnp.concatenate([v[cap:] for v in both], axis=0).astype(bf16)
        low = (
            trans_right(xs[:, :wide], at[0]) + trans_right(xs[:, wide:], at[1])
        ).astype(bf16)
        lanes = lax.broadcasted_iota(jnp.int32, (count, 2 * rank), 1)
        low_gate = jnp.where(lanes < rank, low, jnp.zeros_like(low))
        low_up = jnp.where(lanes < rank, jnp.zeros_like(low), low)
        for lo in range(0, hidden, 256):
            hi = min(lo + 256, hidden)
            gate = trans_right(xs[...], wg[lo:hi]) + trans_right(low_gate, bt[lo:hi])
            upward = trans_right(xs[...], wu[lo:hi]) + trans_right(low_up, bt[lo:hi])
            hidden_grad = trans_right(ds[...], wd[lo:hi])
            sig = 1.0 / (1.0 + jnp.exp(-gate))
            gg[:, lo:hi] = (hidden_grad * upward * sig * (1.0 + gate * (1.0 - sig))).astype(bf16)
            gu[:, lo:hi] = (hidden_grad * gate * sig).astype(bf16)
        back = jnp.where(
            lanes < rank,
            jnp.dot(gg[...], bt[...], preferred_element_type=f32),
            jnp.dot(gu[...], bt[...], preferred_element_type=f32),
        ).astype(bf16)
        tile = wide // 4

        def columns(t, carry):
            sides = []
            for side in range(2):
                cols = pl.ds(pl.multiple_of(side * wide + t * tile, tile), tile)
                inner = pl.ds(pl.multiple_of(t * tile, tile), tile)
                sides.append(
                    jnp.dot(gg[...], wg[:, cols], preferred_element_type=f32)
                    + jnp.dot(gu[...], wu[:, cols], preferred_element_type=f32)
                    + jnp.dot(back, at[side, :, inner], preferred_element_type=f32)
                )
            for source in range(PLANE):
                these = slice(source * cap, (source + 1) * cap)
                y[b, source, :, inner] = jnp.concatenate(
                    [side[these] for side in sides], axis=0
                ).astype(bf16)
            return carry

        lax.fori_loop(0, 4, columns, 0)

        @pl.when(i > 0)
        def _():
            answer(b)

        for n in range(4):
            cols = pl.ds(n * (width // 4), width // 4)
            acc_a[:, cols] += trans_left(back, xs[:, cols])
        of_b = lax.broadcasted_iota(jnp.int32, (hidden, 2 * rank), 1)
        acc_b[...] += jnp.where(of_b < rank, trans_left(gg[...], low), trans_left(gu[...], low))

    def collect(i):
        b = block_at(i)

        def one(step, carry):
            give_came(b, lax.rem(q + step, PLANE)).wait_recv()
            return carry

        lax.fori_loop(1, PLANE, one, 0)
        give_local(b).wait()
        picker = pickers[b].reshape(PLANE * 2 * cap, 2 * tok)
        tile = wide // 2
        for n in range(2):
            cols = pl.ds(n * tile, tile)
            held = ybuf[b, :, :, cols].reshape(PLANE * 2 * cap, tile)
            zstage[b, :, cols] = trans_left(picker, held).astype(jnp.bfloat16)

        @pl.when(b != z)
        def _():
            home(b).start()

    @pl.when(z < last)
    def _():
        begin(up(z))

    @pl.when(z > 0)
    def _():
        begin(down(z))

    for i in range(len(pieces)):
        piece(i).start()
    acc_a[...] = jnp.zeros_like(acc_a)
    acc_b[...] = jnp.zeros_like(acc_b)

    def step(i, carry):
        @pl.when((i >= 1) & (i < planes))
        def _():
            forward(i)

        @pl.when(i < planes)
        def _():
            spread(i)

        @pl.when(i == 1)
        def _():
            for n in range(len(pieces)):
                piece_local(n).wait()
                piece(n).wait()

        @pl.when((i >= 1) & (i <= planes))
        def _():
            expert(i - 1)

        @pl.when(i == planes)
        def _():
            answer(z)

        @pl.when(i >= 3)
        def _():
            collect(i - 2)

        return carry

    lax.fori_loop(0, planes + 2, step, 0)
    collect(0)

    theirs = pl.ds(pl.multiple_of((1 - half) * hidden_half, hidden_half), hidden_half)
    other_cols = pl.ds(pl.multiple_of((1 - half) * wide, wide), wide)
    own_cols = pl.ds(pl.multiple_of(half * wide, wide), wide)
    grads = (
        remote(acc_a.at[:, other_cols], got_a, g_send.at[0], g_recv.at[0], partner),
        remote(acc_b.at[theirs], got_b, g_send.at[1], g_recv.at[1], partner),
    )
    for copy in grads:
        copy.start()
    for copy in grads:
        copy.wait()
    total_a = acc_a[:, own_cols] + got_a[...]
    sum_ag[...] = total_a[:rank]
    sum_au[...] = total_a[rank:]
    total_b = (acc_b[mine] + got_b[...]).T
    sum_bg[...] = total_b[:rank]
    sum_bu[...] = total_b[rank:]

    def add(step, total):
        source = lax.rem(z + step, planes)
        home_came(source).wait_recv()
        return total + zin[source].astype(jnp.float32)

    total = lax.fori_loop(1, planes, add, zstage[z].astype(jnp.float32))
    out_ref[:, :wide] = total[:tok].astype(jnp.bfloat16)
    out_ref[:, wide:] = total[tok:].astype(jnp.bfloat16)

    def finish(b, carry):
        def one(step, inner):
            to = lax.rem(q + step, PLANE)
            part(b, to).wait_send()
            give(b, to).wait_send()
            return inner

        lax.fori_loop(1, PLANE, one, 0)

        @pl.when((b <= z) & (z < last))
        def _():
            sent(up(b))

        @pl.when((b >= z) & (z > 0))
        def _():
            sent(down(b))

        @pl.when(b != z)
        def _():
            home(b).wait_send()

        return carry

    lax.fori_loop(0, planes, finish, 0)


def layer(planes, experts, cap, tokens, cotangent, meta, pieces):
    tok, width = tokens.shape
    hidden_half = pieces[0].shape[0]
    rank = pieces[3].shape[0]
    hidden, wide, count = 2 * hidden_half, width // 2, PLANE * cap
    bf16, f32 = jnp.bfloat16, jnp.float32
    dma = pltpu.SemaphoreType.DMA
    shape = jax.ShapeDtypeStruct
    per_block, per_pair, six = dma((planes,)), dma((planes, PLANE)), dma((len(pieces),))
    return pl.pallas_call(
        functools.partial(layer_kernel, planes, experts, cap),
        out_shape=[
            shape((tok, width), bf16),
            shape((rank, wide), f32),
            shape((rank, wide), f32),
            shape((rank, hidden_half), f32),
            shape((rank, hidden_half), f32),
        ],
        in_specs=[ANY, ANY, VMEM] + [ANY] * len(pieces),
        out_specs=[VMEM] * 5,
        scratch_shapes=[
            pltpu.VMEM((planes, 2 * tok, width), bf16),
            pltpu.VMEM((planes,) + meta.shape, f32),
            pltpu.VMEM((planes, PLANE, 2 * cap, width), bf16),
            pltpu.VMEM((planes, PLANE, 2 * cap, width), bf16),
            pltpu.VMEM((planes, PLANE, 2 * cap, 2 * tok), bf16),
            pltpu.VMEM((hidden, width), bf16),
            pltpu.VMEM((hidden, width), bf16),
            pltpu.VMEM((hidden, width), bf16),
            pltpu.VMEM((2, 2 * rank, wide), bf16),
            pltpu.VMEM((hidden, 2 * rank), bf16),
            pltpu.VMEM((count, width), bf16),
            pltpu.VMEM((count, width), bf16),
            pltpu.VMEM((count, hidden), bf16),
            pltpu.VMEM((count, hidden), bf16),
            pltpu.VMEM((2 * rank, width), f32),
            pltpu.VMEM((hidden, 2 * rank), f32),
            pltpu.VMEM((2 * rank, wide), f32),
            pltpu.VMEM((hidden_half, 2 * rank), f32),
            pltpu.VMEM((planes, PLANE, 2 * cap, wide), bf16),
            pltpu.VMEM((planes, PLANE, 2 * cap, wide), bf16),
            pltpu.VMEM((planes, 2 * tok, wide), bf16),
            pltpu.VMEM((planes, 2 * tok, wide), bf16),
            dma((2,)),
            six,
            six,
            six,
        ]
        + [per_block] * 6
        + [per_pair, per_pair, per_block]
        + [per_pair, per_pair, per_block]
        + [per_block, per_block, dma((2,)), dma((2,))],
        compiler_params=pltpu.CompilerParams(
            collective_id=0, has_side_effects=True, vmem_limit_bytes=62 * 2**20
        ),
        name="layer",
    )(tokens, cotangent, meta, *pieces)


def on_device(
    tokens,
    cotangent,
    token_experts,
    routing_weight_cache,
    gate_weight,
    up_weight,
    down_weight,
    gate_adapter_input,
    gate_adapter_output,
    up_adapter_input,
    up_adapter_output,
):
    n_devices = lax.axis_size("expert")
    n_experts = n_devices // 2
    planes = n_experts // PLANE
    tok, width = tokens.shape
    top = token_experts.shape[1]
    slot_cap = 2 * max(2, 9 * tok * top // (16 * n_experts) + 1)
    slot_cap = (slot_cap + 7) // 8 * 8
    rank = gate_adapter_input.shape[2]

    named = token_experts[None, :, :] == jnp.arange(n_experts, dtype=jnp.int32)[:, None, None]
    chosen = jnp.any(named, axis=2).astype(jnp.float32)
    earlier = (
        lax.broadcasted_iota(jnp.int32, (tok, tok), 0)
        < lax.broadcasted_iota(jnp.int32, (tok, tok), 1)
    ).astype(jnp.float32)
    slots = jnp.dot(chosen, earlier, preferred_element_type=jnp.float32)
    slots = jnp.where(chosen > 0, slots, -1.0)
    weights = jnp.sum(jnp.where(named, routing_weight_cache[None, :, :], 0.0), axis=2)
    meta = jnp.concatenate([slots, weights], axis=0)

    pieces = (
        gate_weight[0].T,
        up_weight[0].T,
        down_weight[0],
        gate_adapter_input[0].T,
        up_adapter_input[0].T,
        jnp.concatenate([gate_adapter_output[0], up_adapter_output[0]], axis=0).T,
    )
    grad_tokens, sum_ag, sum_au, sum_bg, sum_bu = layer(
        planes, n_experts, slot_cap, tokens, cotangent, meta, pieces
    )
    return (
        grad_tokens,
        sum_ag.T[None],
        sum_bg[None],
        sum_au.T[None],
        sum_bu[None],
    )


def solution(mesh):
    in_specs = (
        P(("groups", "expert"), None),
        P(("groups", "expert"), None),
        P(("groups", "expert"), None),
        P(("groups", "expert"), None),
        P("expert", None, None),
        P("expert", None, None),
        P("expert", None, None),
        P("expert", None, None),
        P("expert", None, None),
        P("expert", None, None),
        P("expert", None, None),
    )
    out_specs = (
        P(("groups", "expert"), None),
        P(("groups", "expert"), None, None),
        P(("groups", "expert"), None, None),
        P(("groups", "expert"), None, None),
        P(("groups", "expert"), None, None),
    )
    return jax.shard_map(
        on_device, mesh=mesh, in_specs=in_specs, out_specs=out_specs, check_vma=False
    )
```
